256 devices in a mesh: ex: 16 (over x_hi, y, core), tp: 16 (over z, x_lo).
Axes of the slice: x: 4 (x_hi: 2, x_lo: 2; x = x_hi * 2 + x_lo), y: 4, z: 8, core: 2. Of those that a mesh axis runs over, the one named last changes fastest.
Arguments:
- act: bfloat16 [4096, 7168], P('ex', 'tp'), may hold values from -6 to 6
- grad_out: bfloat16 [4096, 7168], P('ex'), may hold values from -6 to 6
- q_cols: float32 [128, 8], replicated, may hold values from -0.09375 to 0.09375
- example_order: int32 [128], replicated, may hold values from 0 to 127, each once
- segment: int32 [4096], P('ex'), may hold values from 0 to 127, never falling along the last dimension, each value on 1 to 48 neighbouring positions
Outputs:
- sketch: bfloat16 [7168, 8, 7168], P('tp', None, 'ex')
The draws below stay inside these ranges and needn't reach their ends.
Inputs may be any that keep to these rules, and one draw needn't show every extreme that they name: example_order holds each number of 0 to 127 once. segment never falls along the tokens; each example has 1 to 48 tokens.
All inputs are finite; a program needn't handle non-finite values.
Results may differ from the reference program's by a relative error of at most 0.0049.
Values may be sent and summed in bfloat16 or wider, within the bound.
A program may use at most 128 MiB of HBM per device.

```python
import math
import jax
import jax.numpy as jnp
import numpy as np
from jax import lax

D = 7168
K = 8
SEQ_LEN = 32
TOKENS = 4096
EXAMPLES = 128


def block_scale(own_key, shape, shards, smallest, top_value):
    factor_of, own = 1.0, jax.random.fold_in(own_key, 6)
    for axis_at, blocks in shards:
        heights = jnp.exp(jax.random.uniform(jax.random.fold_in(own, axis_at), (blocks,), jnp.float32, smallest / len(shards), top_value / len(shards)))
        factor_of = factor_of * jnp.repeat(heights, shape[axis_at] // blocks).reshape([-1 if axis == axis_at else 1 for axis in range(len(shape))])
    return factor_of


def length_profile(number_of, total, limit, skew):
    loads = [(1 << 20) // math.isqrt(grade ** skew) + 1 for grade in range(2, number_of + 1)]
    spare, given = total - limit - (number_of - 1), [1] * (number_of - 1)
    while spare > 0:
        free = [i for i in range(number_of - 1) if given[i] < limit]
        pool, budget = sum([loads[i] for i in free]), spare
        for i in free:
            addition = min(limit - given[i], max(1, budget * loads[i] // pool), spare)
            given[i] = given[i] + addition
            spare = spare - addition
    return np.array([limit] + given)


def uneven(key, amount, total, reach, slope):
    if amount == 2:
        one = jax.random.randint(key, (), max(1, total - reach), min(reach, total - 1) + 1)
        return jnp.stack([one, total - one])
    sizes = jnp.asarray(length_profile(amount, total, reach, slope), jnp.int32)
    pairs = (amount - 1) // 2
    source_of, receiver = sizes[1:1 + 2 * pairs:2], sizes[2:2 + 2 * pairs:2]
    slack = jnp.minimum(source_of - 1, reach - receiver)
    passed = jax.random.randint(jax.random.fold_in(key, 1), (pairs,), 0, 1 << 20) % (slack + 1)
    sizes = sizes.at[1:1 + 2 * pairs:2].set(source_of - passed).at[2:2 + 2 * pairs:2].set(receiver + passed)
    return sizes[jax.random.permutation(jax.random.fold_in(key, 2), amount)]


def noise(stream_key, shape, width, bound, pieces=(), kind=jnp.bfloat16):
    drawn = jax.random.normal(stream_key, shape, jnp.float32) * width
    if len(pieces) > 0:
        drawn = block_scale(stream_key, shape, pieces, -0.22, 0.18) * drawn
    return jnp.clip(drawn, min=-bound, max=bound).astype(kind)


def setup_inputs(seed: int = 0) -> dict:
    key_of = jax.random.split(jax.random.key(seed), 6)
    return {
        "act": noise(key_of[0], (TOKENS, D), 1.0, 6.0, ((0, 16), (1, 16))),
        "grad_out": noise(key_of[1], (TOKENS, D), 1.0, 6.0, ((0, 16),)),
        "q_cols": noise(key_of[2], (EXAMPLES, K), TOKENS ** -0.5, 0.09375, (), jnp.float32),
        "example_order": jax.random.permutation(key_of[3], EXAMPLES).astype(jnp.int32),
        "segment": jnp.searchsorted(jnp.cumsum(uneven(key_of[4], EXAMPLES, TOKENS, SEQ_LEN + SEQ_LEN // 2, 0)), jnp.arange(TOKENS), side="right").astype(jnp.int32),
    }


def reference(act, grad_out, q_cols, example_order, segment):
    weight = jnp.take(q_cols, jnp.take(example_order, segment, axis=0), axis=0)
    act_t = act.T

    def one_column(column):
        scaled = (grad_out.astype(jnp.float32) * column[:, None]).astype(jnp.bfloat16)
        return jnp.dot(act_t, scaled, preferred_element_type=jnp.float32).astype(jnp.bfloat16)

    stacked = lax.map(one_column, weight.T)
    return jnp.transpose(stacked, (1, 0, 2))
```

```python
import jax
import jax.numpy as jnp
from jax import lax
from jax.experimental import pallas as pl
from jax.experimental.pallas import tpu as pltpu
from jax.sharding import PartitionSpec as P

MESH = pl.DeviceIdType.MESH
BF16, F32 = jnp.bfloat16, jnp.float32
NX, NY, NZ = 2, 4, 8
GROUPS = NX * NY
TOK = 256
WIN = 448
SLAB = 896
HALF = 512
MSG = 480
SHARE = TOK // 4
K = 8
BLOCK = 64


def ring(q):
    return q + q // 2 - 2 * (q // 3)


def kernel(
    act, grad, q_cols, order, segment, out,
    a_buf, g_buf, h_buf, rhs, acc, stage,
    local_sem, out_sem,
    a_send, a_recv, as_send, as_recv, d_send, d_recv, z_send, z_recv, h_send, h_recv,
):
    e, t = lax.axis_index("ex"), lax.axis_index("tp")
    xh, y, c = e // 8, (e // 2) % 4, e % 2
    z, xl = t // 2, t % 2
    share = z % 4

    def dev(dx=0, dy=0, dz=0, dc=0):
        return (
            ((xh + dx) % NX) * 8 + ((y + dy) % NY) * 2 + (c + dc) % 2,
            ((z + dz) % NZ) * 2 + xl,
        )

    def remote(src, dst, send, recv, to):
        return pltpu.make_async_remote_copy(
            src_ref=src, dst_ref=dst, send_sem=send, recv_sem=recv,
            device_id=to, device_id_type=MESH,
        )

    barrier = pltpu.get_barrier_semaphore()
    peers = [dev(dx, dy) for dy in range(NY) for dx in range(NX) if (dx, dy) != (0, 0)]
    peers += [dev(dz=1), dev(dz=-1), dev(dc=1)]
    for peer in peers:
        pl.semaphore_signal(barrier, inc=1, device_id=peer, device_id_type=MESH)

    own = pl.ds(0, TOK)
    other = pl.ds(TOK, TOK)
    act_in = pltpu.make_async_copy(act, a_buf.at[0, pl.ds(0, WIN), own], local_sem.at[0])
    act_in.start()
    slab = pl.multiple_of(SLAB * (4 * xh + y), 128)
    grad_in = pltpu.make_async_copy(grad.at[:, pl.ds(slab, SLAB)], g_buf.at[0], local_sem.at[1])
    grad_in.start()

    labels = lax.broadcasted_iota(jnp.int32, (128, TOK), 0)
    in_example = (jnp.broadcast_to(segment[...], (128, TOK)) == labels).astype(F32).astype(BF16)
    order_rows = jnp.broadcast_to(order[...].astype(F32), (16, 128)).astype(BF16)
    rows = jnp.dot(order_rows, in_example, preferred_element_type=F32)
    picked = jnp.broadcast_to(rows[0:1, :], (128, TOK)) == labels.astype(F32)
    q = q_cols[...]
    q1 = q.astype(BF16).astype(F32)
    q2 = (q - q1).astype(BF16).astype(F32)
    q3 = q - q1 - q2
    parts = jnp.concatenate([q1, q2, q3, jnp.zeros_like(q)], axis=0).astype(BF16)
    weights = jnp.dot(parts, picked.astype(F32).astype(BF16), preferred_element_type=F32)
    a_buf[0, pl.ds(WIN, MSG - WIN), own] = weights.astype(BF16)
    act_in.wait()

    pl.semaphore_wait(barrier, len(peers))

    def direct(r):
        dx, dy = r % 2, ring(r // 2)
        to_x, to_y = (xh + dx) % NX, (y - dy + NY) % NY
        lanes = pl.ds(pl.multiple_of(SLAB * (4 * to_x + to_y), 128), SLAB)
        mine = pl.ds(pl.multiple_of(SHARE * share, SHARE), SHARE)
        return remote(
            grad.at[mine, lanes], g_buf.at[r, mine, :], d_send.at[r], d_recv.at[r],
            (to_x * 8 + to_y * 2 + c, t),
        )

    def along_z(r, hop, way):
        if hop == 0:
            at = pl.ds(pl.multiple_of(SHARE * share, SHARE), SHARE)
        else:
            of = (share + (3 if way == 0 else 1)) % 4
            at = pl.ds(pl.multiple_of(SHARE * of + (SHARE // 2) * way, SHARE // 2), SHARE // 2)
        part = g_buf.at[r, at, :]
        i = hop * 2 + way
        return remote(part, part, z_send.at[r, i], z_recv.at[r, i], dev(dz=1 if way == 0 else -1))

    def to_sibling(r):
        lanes = pl.ds(pl.multiple_of(384 * (1 - c), 128), HALF)
        return remote(g_buf.at[r, :, lanes], h_buf.at[r], h_send.at[r], h_recv.at[r], dev(dc=1))

    def act_whole(i):
        src, dst, to = [
            (0, 1, dev(dx=1)),
            (0, 4, dev(dy=1)), (0, 2, dev(dy=-1)),
            (1, 5, dev(dy=1)), (1, 3, dev(dy=-1)),
        ][i]
        return remote(a_buf.at[src, :, own], a_buf.at[dst, :, own], a_send.at[i], a_recv.at[i], to)

    def act_half(i):
        src, dst, to, at = [
            (4, 6, dev(dy=1), 0), (2, 6, dev(dy=-1), MSG // 2),
            (5, 7, dev(dy=1), 0), (3, 7, dev(dy=-1), MSG // 2),
        ][i]
        at = pl.ds(at, MSG // 2)
        return remote(
            a_buf.at[src, at, own], a_buf.at[dst, at, own], a_send.at[5 + i], a_recv.at[5 + i], to
        )

    def act_sibling(r):
        return remote(
            a_buf.at[r, :, own], a_buf.at[r, :, other], as_send.at[r], as_recv.at[r], dev(dc=1)
        )

    act_whole(0).start()
    lax.fori_loop(1, GROUPS, lambda r, _: (direct(r).start(), 0)[1], 0)
    act_whole(1).start()
    act_whole(2).start()
    act_sibling(0).start()
    grad_in.wait()
    to_sibling(0).start()

    rhs[...] = jnp.zeros_like(rhs)
    acc[...] = jnp.zeros_like(acc)

    def load_rhs(r):
        @pl.when(c == 0)
        def _():
            rhs[0:TOK, :] = g_buf[r, :, 0:HALF]
            rhs[TOK:, :] = h_buf[r]

        @pl.when(c == 1)
        def _():
            rhs[0:TOK, 0:WIN] = g_buf[r, :, SLAB - WIN:SLAB]
            rhs[TOK:, 0:WIN] = h_buf[r, :, HALF - WIN:HALF]

    def product(r, i):
        w = a_buf[r, WIN:WIN + 32, :].astype(F32)
        w = w[0:8] + w[8:16] + w[16:24]
        part = a_buf[r, pl.ds(i * BLOCK, BLOCK), :].astype(F32)
        left = (part[:, None, :] * w[None, :, :]).reshape(BLOCK * K, 2 * TOK).astype(BF16)
        return jnp.dot(left, rhs[...], preferred_element_type=F32)

    def compute(r):
        load_rhs(r)
        for i in range(WIN // BLOCK):
            acc[pl.ds(i * BLOCK * K, BLOCK * K), :] += product(r, i)

    def out_copy(i):
        at = pl.ds(i * BLOCK, BLOCK)
        return pltpu.make_async_copy(stage.at[at], out.at[at], out_sem.at[i])

    def compute_last(r):
        load_rhs(r)
        for i in range(WIN // BLOCK):
            total = acc[pl.ds(i * BLOCK * K, BLOCK * K), :] + product(r, i)
            stage[pl.ds(i * BLOCK, BLOCK)] = total[:, 0:WIN].reshape(BLOCK, K, WIN).astype(BF16)
            out_copy(i).start()

    def tick(n, _):
        @pl.when(n <= 7)
        def _():
            direct(n).wait_recv()
            along_z(n, 0, 0).start()
            along_z(n, 0, 1).start()

        @pl.when(n == 1)
        def _():
            act_whole(0).wait_recv()
            act_whole(3).start()
            act_whole(4).start()
            act_sibling(1).start()

        @pl.when(n == 2)
        def _():
            act_whole(1).wait_recv()
            act_half(0).start()
            act_sibling(4).start()
            act_whole(2).wait_recv()
            act_half(1).start()
            act_sibling(2).start()

        @pl.when(n == 4)
        def _():
            act_whole(3).wait_recv()
            act_half(2).start()
            act_sibling(5).start()
            act_whole(4).wait_recv()
            act_half(3).start()
            act_sibling(3).start()

        @pl.when(n == 7)
        def _():
            act_half(0).wait_recv()
            act_half(1).wait_recv()
            act_sibling(6).start()

        @pl.when(n == 8)
        def _():
            act_half(2).wait_recv()
            act_half(3).wait_recv()
            act_sibling(7).start()

        @pl.when((n >= 2) & (n <= 8))
        def _():
            r = n - 1
            along_z(r, 0, 0).wait_recv()
            along_z(r, 1, 0).start()
            along_z(r, 0, 1).wait_recv()
            along_z(r, 1, 1).start()

        @pl.when((n >= 3) & (n <= 9))
        def _():
            r = n - 2
            along_z(r, 1, 0).wait_recv()
            along_z(r, 1, 1).wait_recv()
            to_sibling(r).start()

        @pl.when((n == 1) | (n >= 4))
        def _():
            r = jnp.where(n == 1, 0, n - 3)
            act_sibling(r).wait_recv()
            to_sibling(r).wait_recv()
            compute(r)

        return 0

    lax.fori_loop(1, GROUPS + 2, tick, 0)
    act_sibling(GROUPS - 1).wait_recv()
    to_sibling(GROUPS - 1).wait_recv()
    compute_last(GROUPS - 1)

    for i in range(5):
        act_whole(i).wait_send()
    for i in range(4):
        act_half(i).wait_send()

    def drain(r, _):
        act_sibling(r).wait_send()
        to_sibling(r).wait_send()

        @pl.when(r > 0)
        def _():
            direct(r).wait_send()
            for hop in range(2):
                for way in range(2):
                    along_z(r, hop, way).wait_send()

        return 0

    lax.fori_loop(0, GROUPS, drain, 0)
    for i in range(WIN // BLOCK):
        out_copy(i).wait()


def local(act, grad_out, q_cols, example_order, segment):
    dma = pltpu.SemaphoreType.DMA
    return pl.pallas_call(
        kernel,
        out_shape=jax.ShapeDtypeStruct((WIN, K, WIN), BF16),
        in_specs=[pl.BlockSpec(memory_space=pl.ANY)] * 2 + [pl.BlockSpec(memory_space=pltpu.VMEM)] * 3,
        out_specs=pl.BlockSpec(memory_space=pl.ANY),
        scratch_shapes=[
            pltpu.VMEM((GROUPS, MSG, 2 * TOK), BF16),
            pltpu.VMEM((GROUPS, TOK, SLAB), BF16),
            pltpu.VMEM((GROUPS, TOK, HALF), BF16),
            pltpu.VMEM((2 * TOK, HALF), BF16),
            pltpu.VMEM((WIN * K, HALF), F32),
            pltpu.VMEM((WIN, K, WIN), BF16),
            dma((2,)), dma((WIN // BLOCK,)),
            dma((9,)), dma((9,)), dma((GROUPS,)), dma((GROUPS,)),
            dma((GROUPS,)), dma((GROUPS,)), dma((GROUPS, 4)), dma((GROUPS, 4)),
            dma((GROUPS,)), dma((GROUPS,)),
        ],
        compiler_params=pltpu.CompilerParams(
            collective_id=1, has_side_effects=True, vmem_limit_bytes=48 * 1024 * 1024
        ),
    )(act.T, grad_out, q_cols.T, example_order[None, :], segment[None, :])


def solution(mesh):
    in_specs = (P("ex", "tp"), P("ex", None), P(), P(), P("ex"))
    out_specs = P("tp", None, "ex")
    return jax.shard_map(local, mesh=mesh, in_specs=in_specs, out_specs=out_specs, check_vma=False)
```

```python
import jax
import jax.numpy as jnp
from jax import lax
from jax.experimental import pallas as pl
from jax.experimental.pallas import tpu as pltpu
from jax.sharding import PartitionSpec as P

MESH = pl.DeviceIdType.MESH
BF16, F32 = jnp.bfloat16, jnp.float32
NX, NY, NZ = 2, 4, 8
TOK = 256
WIN = 448
SLAB = 896
HALF = 512
MSG = 480
K = 8
BLOCK = 112
WIDE = 224
SOURCES = ((0, 0), (0, 1), (0, 3), (1, 0), (1, 1), (1, 3), (0, 2), (1, 2))
GROUPS = len(SOURCES)
WHOLE = (3,)
SPLIT = (2, 4, 7)
GO, GET = True, False
FIRST = (
    (GO, 'act_core', 0),
    (GO, 'columns', 0),
    (GO, 'direct', 4),
    (GO, 'direct', 2),
    (GO, 'act', 0),
    (GO, 'direct', 7),
    (GO, 'direct', 5),
    (GO, 'act', 1),
    (GO, 'direct', 1),
    (GO, 'act', 2),
)
STEPS = (
    ((), 0, 0),
    ((
        (GET, 'act_core', 0),
        (GET, 'columns', 0),
    ), 0, 1),
    ((
        (GET, 'direct', 2),
        (GO, 'z_first', 2, 1),
        (GO, 'z_first', 2, 0),
        (GET, 'direct', 4),
        (GO, 'z_first', 4, 0),
        (GO, 'z_first', 4, 1),
        (GO, 'direct', 3),
        (GO, 'direct', 6),
        (GET, 'z_first', 2, 1),
        (GET, 'z_first', 2, 0),
        (GO, 'z_second', 2, 0),
        (GO, 'z_second', 2, 1),
        (GET, 'direct', 1),
        (GO, 'z_first', 1, 0),
        (GO, 'z_first', 1, 1),
        (GET, 'z_first', 4, 0),
        (GET, 'z_first', 4, 1),
        (GO, 'z_second', 4, 1),
        (GO, 'z_second', 4, 0),
        (GET, 'z_second', 2, 0),
        (GET, 'z_second', 2, 1),
        (GO, 'x_lo', 2),
        (GET, 'act', 0),
        (GO, 'act_core', 3),
        (GO, 'act', 4),
        (GET, 'direct', 7),
        (GO, 'act', 3),
        (GO, 'z_first', 7, 0),
        (GO, 'z_first', 7, 1),
        (GET, 'act_core', 3),
        (GET, 'z_first', 1, 0),
        (GET, 'z_first', 1, 1),
        (GO, 'z_second', 1, 1),
        (GO, 'z_second', 1, 0),
        (GET, 'z_second', 4, 1),
        (GET, 'z_second', 4, 0),
        (GO, 'x_lo', 4),
        (GET, 'act', 1),
        (GO, 'act_core', 2),
        (GET, 'act', 2),
        (GO, 'act_core', 1),
        (GO, 'act_half', 0),
        (GO, 'act_half', 1),
        (GET, 'direct', 5),
        (GO, 'z_first', 5, 0),
        (GO, 'z_first', 5, 1),
        (GET, 'z_first', 7, 0),
        (GET, 'z_first', 7, 1),
        (GO, 'z_second', 7, 1),
        (GO, 'z_second', 7, 0),
        (GET, 'act_core', 2),
        (GET, 'act_core', 1),
        (GET, 'z_second', 1, 1),
        (GET, 'z_second', 1, 0),
        (GO, 'columns', 1),
    ), 1, 0),
    ((
        (GET, 'x_lo', 2),
        (GO, 'columns', 2),
        (GET, 'direct', 6),
        (GO, 'z_first', 6, 0),
        (GO, 'z_first', 6, 1),
    ), 2, 0),
    ((
        (GET, 'columns', 1),
        (GET, 'z_first', 5, 0),
        (GET, 'z_first', 5, 1),
        (GO, 'z_second', 5, 0),
        (GO, 'z_second', 5, 1),
    ), 1, 1),
    ((
        (GET, 'columns', 2),
        (GET, 'z_second', 7, 1),
        (GET, 'z_second', 7, 0),
        (GO, 'x_lo', 7),
    ), 2, 1),
    ((
        (GET, 'z_first', 6, 0),
        (GET, 'z_first', 6, 1),
        (GO, 'z_second', 6, 1),
        (GO, 'z_second', 6, 0),
        (GET, 'act', 4),
        (GO, 'act_core', 4),
        (GET, 'act', 3),
        (GO, 'act_core', 5),
        (GO, 'act_half', 3),
        (GO, 'act_half', 2),
        (GET, 'x_lo', 4),
        (GO, 'columns', 4),
    ), 4, 0),
    ((
        (GET, 'z_second', 5, 0),
        (GET, 'z_second', 5, 1),
        (GO, 'columns', 5),
    ), 5, 0),
    ((
        (GET, 'act_core', 4),
        (GET, 'act_core', 5),
        (GET, 'direct', 3),
        (GO, 'columns', 3),
        (GET, 'columns', 4),
    ), 4, 1),
    ((
        (GET, 'z_second', 6, 1),
        (GET, 'z_second', 6, 0),
        (GO, 'columns', 6),
        (GET, 'act_half', 0),
        (GET, 'act_half', 1),
        (GO, 'act_core', 6),
        (GET, 'columns', 5),
    ), 5, 1),
    ((
        (GET, 'columns', 3),
        (GET, 'x_lo', 7),
        (GO, 'columns', 7),
    ), 3, 2),
    ((
        (GET, 'act_half', 3),
        (GET, 'act_half', 2),
        (GO, 'act_core', 7),
        (GET, 'columns', 6),
        (GET, 'act_core', 6),
        (GET, 'columns', 7),
    ), 6, 2),
    ((
        (GET, 'act_core', 7),
    ), 7, 2),
)

def kernel(
    act, grad, q_cols, order, segment, out,
    a_buf, g_buf, h_buf, rhs, acc, q_buf, order_buf, segment_buf, local_sem,
    a_send, a_recv, as_send, as_recv, d_send, d_recv, z_send, z_recv, x_send, x_recv, h_send, h_recv,
):
    e, t = lax.axis_index("ex"), lax.axis_index("tp")
    xh, y, c = e // 8, (e // 2) % 4, e % 2
    z, xl = t // 2, t % 2
    share = z % 4

    def dev(dx=0, dy=0, dz=0, dc=0, dl=0):
        return (
            ((xh + dx) % NX) * 8 + ((y + dy + NY) % NY) * 2 + (c + dc) % 2,
            ((z + dz + NZ) % NZ) * 2 + (xl + dl) % 2,
        )

    def remote(src, dst, send, recv, to):
        return pltpu.make_async_remote_copy(
            src_ref=src, dst_ref=dst, send_sem=send, recv_sem=recv,
            device_id=to, device_id_type=MESH,
        )

    barrier = pltpu.get_barrier_semaphore()
    peers = [dev(dx, dy, dl=dx) for dx, dy in SOURCES[1:]]
    peers += [dev(dx=1), dev(dl=1), dev(dz=1), dev(dz=-1), dev(dc=1)]
    for peer in peers:
        pl.semaphore_signal(barrier, inc=1, device_id=peer, device_id_type=MESH)

    own = pl.ds(0, TOK)
    other = pl.ds(TOK, TOK)
    slab = pl.multiple_of(SLAB * (4 * xh + y), 128)
    loads = [
        pltpu.make_async_copy(src, dst, local_sem.at[i])
        for i, (src, dst) in enumerate([
            (order, order_buf), (segment, segment_buf), (q_cols, q_buf),
            (act, a_buf.at[0, pl.ds(0, WIN), own]),
            (grad.at[:, pl.ds(slab, SLAB)], g_buf.at[0]),
        ])
    ]
    for load in loads:
        load.start()
    rhs[...] = jnp.zeros_like(rhs)
    acc[...] = jnp.zeros_like(acc)
    for load in loads[:3]:
        load.wait()

    labels = lax.broadcasted_iota(jnp.int32, (128, TOK), 0)
    in_example = (jnp.broadcast_to(segment_buf[...], (128, TOK)) == labels).astype(F32).astype(BF16)
    order_rows = jnp.broadcast_to(order_buf[...].astype(F32), (16, 128)).astype(BF16)
    rows = jnp.dot(order_rows, in_example, preferred_element_type=F32)
    picked = jnp.broadcast_to(rows[0:1, :], (128, TOK)) == labels.astype(F32)
    q = q_buf[...]
    q1 = q.astype(BF16).astype(F32)
    q2 = (q - q1).astype(BF16).astype(F32)
    q3 = q - q1 - q2
    parts = jnp.concatenate([q1, q2, q3, jnp.zeros_like(q)], axis=0).astype(BF16)
    weights = jnp.dot(parts, picked.astype(F32).astype(BF16), preferred_element_type=F32)
    a_buf[0, pl.ds(WIN, MSG - WIN), own] = weights.astype(BF16)
    loads[3].wait()

    pl.semaphore_wait(barrier, len(peers))

    def quarter(r, q, side, half=None):
        if r in WHOLE:
            return pl.ds(0, TOK)
        rows = TOK // 8 if r in SPLIT else TOK // 4
        at = q * rows + (side * (TOK // 2) if r in SPLIT else 0)
        if half is not None:
            rows = rows // 2
            at = at + half * rows
        return pl.ds(pl.multiple_of(at, rows), rows)

    def direct(r):
        dx, dy = SOURCES[r]
        to_x, to_y = (xh + dx) % NX, (y - dy + NY) % NY
        lanes = pl.ds(pl.multiple_of(SLAB * (4 * to_x + to_y), 128), SLAB)
        rows = quarter(r, share, (xl + dx) % 2)
        return remote(
            grad.at[rows, lanes], g_buf.at[r, rows, :], d_send.at[r], d_recv.at[r], dev(dx, -dy, dl=dx)
        )

    def direct_in(r):
        part = g_buf.at[r, quarter(r, share, xl), :]
        return remote(part, part, d_send.at[r], d_recv.at[r], dev(dc=1))

    def along_z(r, hop, way):
        if hop == 0:
            at = quarter(r, share, xl)
        else:
            at = quarter(r, (share + (3 if way == 0 else 1)) % 4, xl, way)
        part = g_buf.at[r, at, :]
        i = hop * 2 + way
        return remote(part, part, z_send.at[r, i], z_recv.at[r, i], dev(dz=1 if way == 0 else -1))

    def to_x_lo(r):
        half = TOK // 2
        part = g_buf.at[r, pl.ds(pl.multiple_of(xl * half, half), half), :]
        return remote(part, part, x_send.at[r], x_recv.at[r], dev(dl=1))

    def to_sibling(r):
        lanes = pl.ds(pl.multiple_of(384 * (1 - c), 128), HALF)
        return remote(g_buf.at[r, :, lanes], h_buf.at[r], h_send.at[r], h_recv.at[r], dev(dc=1))

    def act_whole(i):
        src, dst, to = [
            (0, 3, dev(dx=1)),
            (0, 2, dev(dy=1)), (0, 1, dev(dy=-1)),
            (3, 5, dev(dy=1)), (3, 4, dev(dy=-1)),
        ][i]
        return remote(a_buf.at[src, :, own], a_buf.at[dst, :, own], a_send.at[i], a_recv.at[i], to)

    def act_half(i):
        src, dst, to, at = [
            (2, 6, dev(dy=1), 0), (1, 6, dev(dy=-1), MSG // 2),
            (5, 7, dev(dy=1), 0), (4, 7, dev(dy=-1), MSG // 2),
        ][i]
        at = pl.ds(at, MSG // 2)
        return remote(
            a_buf.at[src, at, own], a_buf.at[dst, at, own], a_send.at[5 + i], a_recv.at[5 + i], to
        )

    def act_sibling(r):
        return remote(
            a_buf.at[r, :, own], a_buf.at[r, :, other], as_send.at[r], as_recv.at[r], dev(dc=1)
        )

    transfers = {
        "direct": direct, "x_lo": to_x_lo, "columns": to_sibling,
        "z_first": lambda r, way: along_z(r, 0, way), "z_second": lambda r, way: along_z(r, 1, way),
        "act": act_whole, "act_half": act_half, "act_core": act_sibling,
    }

    def run(todo):
        for go, name, *which in todo:
            if go:
                transfers[name](*which).start()
            else:
                (direct_in if name == "direct" else transfers[name])(*which).wait_recv()

    run([item for item in FIRST if item[1:] != ("columns", 0)])
    loads[4].wait()
    to_sibling(0).start()

    def load_rhs(r, half):
        at = pl.ds(half * TOK, TOK)

        @pl.when(c == 0)
        def _():
            rhs[at, :] = g_buf[r, :, 0:HALF] if half == 0 else h_buf[r]

        @pl.when(c == 1)
        def _():
            rhs[at, 0:WIN] = g_buf[r, :, SLAB - WIN:SLAB] if half == 0 else h_buf[r, :, HALF - WIN:HALF]

    def product(r, row, size, at):
        w = a_buf[r, WIN:WIN + 32, at].astype(F32)
        w = w[0:8] + w[8:16] + w[16:24]
        part = a_buf[r, pl.ds(row, size), at].astype(F32)
        left = (part[:, None, :] * w[None, :, :]).astype(BF16).reshape(size * K, at.size)
        return jnp.dot(left, rhs[at, :], preferred_element_type=F32)

    def add(r, size, at):
        for row in range(0, WIN, size):
            acc[pl.ds(row * K, size * K), :] += product(r, row, size, at)

    def step(n, _):
        for i, (todo, _, _) in enumerate(STEPS[:-1]):
            if todo:
                pl.when(n == i)(lambda todo=todo: run(todo))
        r = sum(jnp.where(n == i, r, 0) for i, (_, r, _) in enumerate(STEPS[:-1]))
        mode = sum(jnp.where(n == i, mode, 0) for i, (_, _, mode) in enumerate(STEPS[:-1]))

        @pl.when(mode != 1)
        def _():
            load_rhs(r, 0)

        @pl.when(mode != 0)
        def _():
            load_rhs(r, 1)

        @pl.when(mode == 2)
        def _():
            add(r, WIDE, pl.ds(0, 2 * TOK))

        @pl.when(mode != 2)
        def _():
            add(r, BLOCK, pl.ds(pl.multiple_of(mode * TOK, TOK), TOK))

        return 0

    lax.fori_loop(0, len(STEPS) - 1, step, 0)
    todo, r, mode = STEPS[-1]
    run(todo)
    at = (own, other, pl.ds(0, 2 * TOK))[mode]
    if mode != 1:
        load_rhs(r, 0)
    if mode != 0:
        load_rhs(r, 1)
    for row in range(0, WIN, BLOCK):
        total = acc[pl.ds(row * K, BLOCK * K), :] + product(r, row, BLOCK, at)
        out[pl.ds(row, BLOCK)] = total[:, 0:WIN].reshape(BLOCK, K, WIN).astype(BF16)

    for i in range(5):
        act_whole(i).wait_send()
    for i in range(4):
        act_half(i).wait_send()
    for r in range(GROUPS):
        act_sibling(r).wait_send()
        to_sibling(r).wait_send()
        if r > 0:
            direct(r).wait_send()
        if r > 0 and r not in WHOLE:
            for hop in range(2):
                for way in range(2):
                    along_z(r, hop, way).wait_send()
        if r in SPLIT:
            to_x_lo(r).wait_send()


def local(act, grad_out, q_cols, example_order, segment):
    dma = pltpu.SemaphoreType.DMA
    return pl.pallas_call(
        kernel,
        out_shape=jax.ShapeDtypeStruct((WIN, K, WIN), BF16),
        in_specs=[pl.BlockSpec(memory_space=pltpu.HBM)] * 5,
        out_specs=pl.BlockSpec(memory_space=pltpu.VMEM),
        scratch_shapes=[
            pltpu.VMEM((GROUPS, MSG, 2 * TOK), BF16),
            pltpu.VMEM((GROUPS, TOK, SLAB), BF16),
            pltpu.VMEM((GROUPS, TOK, HALF), BF16),
            pltpu.VMEM((2 * TOK, HALF), BF16),
            pltpu.VMEM((WIN * K, HALF), F32),
            pltpu.VMEM((K, 128), F32),
            pltpu.VMEM((1, 128), jnp.int32),
            pltpu.VMEM((1, TOK), jnp.int32),
            dma((5,)),
            dma((9,)), dma((9,)), dma((GROUPS,)), dma((GROUPS,)),
            dma((GROUPS,)), dma((GROUPS,)), dma((GROUPS, 4)), dma((GROUPS, 4)),
            dma((GROUPS,)), dma((GROUPS,)), dma((GROUPS,)), dma((GROUPS,)),
        ],
        compiler_params=pltpu.CompilerParams(
            collective_id=1, has_side_effects=True, vmem_limit_bytes=48 * 1024 * 1024
        ),
    )(act.T, grad_out, q_cols.T, example_order[None, :], segment[None, :])


def solution(mesh):
    in_specs = (P("ex", "tp"), P("ex", None), P(), P(), P("ex"))
    out_specs = P("tp", None, "ex")
    return jax.shard_map(local, mesh=mesh, in_specs=in_specs, out_specs=out_specs, check_vma=False)
```

```python
import jax
import jax.numpy as jnp
from jax import lax
from jax.experimental import pallas as pl
from jax.experimental.pallas import tpu as pltpu
from jax.sharding import PartitionSpec as P

MESH = pl.DeviceIdType.MESH
BF16, F32 = jnp.bfloat16, jnp.float32
NX, NY, NZ = 2, 4, 8
TOK = 256
WIN = 448
SLAB = 896
HALF = 512
MSG = 480
K = 8
BLOCK = 112
WIDE = 224
SOURCES = ((0, 0), (0, 1), (0, 3), (1, 0), (1, 1), (1, 3), (0, 2), (1, 2))
GROUPS = len(SOURCES)
WHOLE = (3,)
SPLIT = (2, 4, 7)
GO, GET = True, False
FIRST = (
    (GO, 'act_core', 0),
    (GO, 'columns', 0),
    (GO, 'direct', 4),
    (GO, 'direct', 2),
    (GO, 'act', 0, 0),
    (GO, 'act', 0, 1),
    (GO, 'direct', 7),
    (GO, 'direct', 5),
    (GO, 'act', 1, 0),
    (GO, 'act', 1, 1),
    (GO, 'direct', 1),
    (GO, 'act', 2, 0),
    (GO, 'act', 2, 1),
)
STEPS = (
    ((), 0, 0),
    ((
        (GET, 'act_core', 0),
        (GET, 'columns', 0),
    ), 0, 1),
    ((
        (GET, 'direct', 2),
        (GO, 'z_first', 2, 1),
        (GO, 'z_first', 2, 0),
        (GET, 'direct', 4),
        (GO, 'z_first', 4, 0),
        (GO, 'z_first', 4, 1),
        (GO, 'direct', 3),
        (GO, 'direct', 6),
        (GET, 'z_first', 2, 1),
        (GET, 'z_first', 2, 0),
        (GO, 'z_second', 2, 0),
        (GO, 'z_second', 2, 1),
        (GET, 'direct', 1),
        (GO, 'z_first', 1, 0),
        (GO, 'z_first', 1, 1),
        (GET, 'z_first', 4, 0),
        (GET, 'z_first', 4, 1),
        (GO, 'z_second', 4, 1),
        (GO, 'z_second', 4, 0),
        (GET, 'z_second', 2, 0),
        (GET, 'z_second', 2, 1),
        (GO, 'x_lo', 2),
        (GET, 'act', 0, 0),
        (GET, 'act', 0, 1),
        (GO, 'act_core', 3),
        (GO, 'act', 4, 0),
        (GO, 'act', 4, 1),
        (GET, 'direct', 7),
        (GO, 'act', 3, 0),
        (GO, 'act', 3, 1),
        (GO, 'z_first', 7, 0),
        (GO, 'z_first', 7, 1),
        (GET, 'act_core', 3),
        (GET, 'z_first', 1, 0),
        (GET, 'z_first', 1, 1),
        (GO, 'z_second', 1, 1),
        (GO, 'z_second', 1, 0),
        (GET, 'z_second', 4, 1),
        (GET, 'z_second', 4, 0),
        (GO, 'x_lo', 4),
        (GET, 'act', 1, 0),
        (GET, 'act', 1, 1),
        (GO, 'act_core', 2),
        (GET, 'act', 2, 0),
        (GET, 'act', 2, 1),
        (GO, 'act_core', 1),
        (GO, 'act_half', 0),
        (GO, 'act_half', 1),
        (GET, 'direct', 5),
        (GO, 'z_first', 5, 0),
        (GO, 'z_first', 5, 1),
        (GET, 'z_first', 7, 0),
        (GET, 'z_first', 7, 1),
        (GO, 'z_second', 7, 1),
        (GO, 'z_second', 7, 0),
        (GET, 'act_core', 2),
        (GET, 'act_core', 1),
        (GET, 'z_second', 1, 1),
        (GET, 'z_second', 1, 0),
        (GO, 'columns', 1),
    ), 1, 0),
    ((
        (GET, 'x_lo', 2),
        (GO, 'columns', 2),
        (GET, 'direct', 6),
        (GO, 'z_first', 6, 0),
        (GO, 'z_first', 6, 1),
    ), 2, 0),
    ((
        (GET, 'columns', 1),
        (GET, 'z_first', 5, 0),
        (GET, 'z_first', 5, 1),
        (GO, 'z_second', 5, 0),
        (GO, 'z_second', 5, 1),
    ), 1, 1),
    ((
        (GET, 'columns', 2),
        (GET, 'z_second', 7, 1),
        (GET, 'z_second', 7, 0),
        (GO, 'x_lo', 7),
    ), 2, 1),
    ((
        (GET, 'z_first', 6, 0),
        (GET, 'z_first', 6, 1),
        (GO, 'z_second', 6, 1),
        (GO, 'z_second', 6, 0),
        (GET, 'act', 4, 0),
        (GET, 'act', 4, 1),
        (GO, 'act_core', 4),
        (GET, 'act', 3, 0),
        (GET, 'act', 3, 1),
        (GO, 'act_core', 5),
        (GO, 'act_half', 3),
        (GO, 'act_half', 2),
        (GET, 'x_lo', 4),
        (GO, 'columns', 4),
    ), 4, 0),
    ((
        (GET, 'z_second', 5, 0),
        (GET, 'z_second', 5, 1),
        (GO, 'columns', 5),
    ), 5, 0),
    ((
        (GET, 'act_core', 4),
        (GET, 'act_core', 5),
        (GET, 'direct', 3),
        (GO, 'columns', 3),
        (GET, 'columns', 4),
    ), 4, 1),
    ((
        (GET, 'z_second', 6, 1),
        (GET, 'z_second', 6, 0),
        (GO, 'columns', 6),
        (GET, 'act_half', 0),
        (GET, 'act_half', 1),
        (GO, 'act_core', 6),
        (GET, 'columns', 5),
    ), 5, 1),
    ((
        (GET, 'columns', 3),
        (GET, 'x_lo', 7),
        (GO, 'columns', 7),
    ), 3, 2),
    ((
        (GET, 'act_half', 3),
        (GET, 'act_half', 2),
        (GO, 'act_core', 7),
        (GET, 'columns', 6),
        (GET, 'act_core', 6),
        (GET, 'columns', 7),
    ), 6, 2),
    ((
        (GET, 'act_core', 7),
    ), 7, 2),
)

def product(a, rhs, row, size, at):
    w = a[WIN:WIN + 32, at].astype(F32)
    w = w[0:8] + w[8:16] + w[16:24]
    left = a[pl.ds(row, size), at].astype(F32)
    left = (left[:, None, :] * w[None, :, :]).astype(BF16).reshape(size * K, at.size)
    return jnp.dot(left, rhs[at, :], preferred_element_type=F32)


def finish(acc, a_last, rhs, out, stage, sem):
    at = (pl.ds(0, TOK), pl.ds(TOK, TOK), pl.ds(0, 2 * TOK))[STEPS[-1][2]]
    copies = []
    for i, row in enumerate(range(0, WIN, BLOCK)):
        total = acc[pl.ds(row * K, BLOCK * K), :] + product(a_last, rhs, row, BLOCK, at)
        stage[pl.ds(row, BLOCK)] = total[:, 0:WIN].reshape(BLOCK, K, WIN).astype(BF16)
        rows = pl.ds(row, BLOCK)
        copies.append(pltpu.make_async_copy(stage.at[rows], out.at[rows], sem.at[i]))
        copies[-1].start()
    for copy in copies:
        copy.wait()


def kernel(
    act, grad, q_cols, order, segment, acc, a_last, rhs,
    a_buf, g_buf, h_buf, q_buf, order_buf, segment_buf, local_sem,
    a_send, a_recv, as_send, as_recv, d_send, d_recv, z_send, z_recv, x_send, x_recv, h_send, h_recv,
):
    e, t = lax.axis_index("ex"), lax.axis_index("tp")
    xh, y, c = e // 8, (e // 2) % 4, e % 2
    z, xl = t // 2, t % 2
    share = z % 4

    def dev(dx=0, dy=0, dz=0, dc=0, dl=0):
        return (
            ((xh + dx) % NX) * 8 + ((y + dy + NY) % NY) * 2 + (c + dc) % 2,
            ((z + dz + NZ) % NZ) * 2 + (xl + dl) % 2,
        )

    def remote(src, dst, send, recv, to):
        return pltpu.make_async_remote_copy(
            src_ref=src, dst_ref=dst, send_sem=send, recv_sem=recv,
            device_id=to, device_id_type=MESH,
        )

    barrier = pltpu.get_barrier_semaphore()
    peers = [dev(dx, dy, dl=dx) for dx, dy in SOURCES[1:]]
    peers += [dev(dx=1), dev(dl=1), dev(dz=1), dev(dz=-1), dev(dc=1)]
    for peer in peers:
        pl.semaphore_signal(barrier, inc=1, device_id=peer, device_id_type=MESH)

    own = pl.ds(0, TOK)
    other = pl.ds(TOK, TOK)
    slab = pl.multiple_of(SLAB * (4 * xh + y), 128)
    loads = [
        pltpu.make_async_copy(src, dst, local_sem.at[i])
        for i, (src, dst) in enumerate([
            (order, order_buf), (segment, segment_buf), (q_cols, q_buf),
            (act, a_buf.at[0, pl.ds(0, WIN), own]),
            (grad.at[:, pl.ds(slab, SLAB)], g_buf.at[0]),
        ])
    ]
    for load in loads:
        load.start()
    def quarter(r, q, side, half=None):
        if r in WHOLE:
            return pl.ds(0, TOK)
        rows = TOK // 8 if r in SPLIT else TOK // 4
        at = q * rows + (side * (TOK // 2) if r in SPLIT else 0)
        if half is not None:
            rows = rows // 2
            at = at + half * rows
        return pl.ds(pl.multiple_of(at, rows), rows)

    def direct(r):
        dx, dy = SOURCES[r]
        to_x, to_y = (xh + dx) % NX, (y - dy + NY) % NY
        lanes = pl.ds(pl.multiple_of(SLAB * (4 * to_x + to_y), 128), SLAB)
        rows = quarter(r, share, (xl + dx) % 2)
        return remote(
            grad.at[rows, lanes], g_buf.at[r, rows, :], d_send.at[r], d_recv.at[r], dev(dx, -dy, dl=dx)
        )

    def direct_in(r):
        part = g_buf.at[r, quarter(r, share, xl), :]
        return remote(part, part, d_send.at[r], d_recv.at[r], dev(dc=1))

    def along_z(r, hop, way):
        if hop == 0:
            at = quarter(r, share, xl)
        else:
            at = quarter(r, (share + (3 if way == 0 else 1)) % 4, xl, way)
        part = g_buf.at[r, at, :]
        i = hop * 2 + way
        return remote(part, part, z_send.at[r, i], z_recv.at[r, i], dev(dz=1 if way == 0 else -1))

    def to_x_lo(r):
        half = TOK // 2
        part = g_buf.at[r, pl.ds(pl.multiple_of(xl * half, half), half), :]
        return remote(part, part, x_send.at[r], x_recv.at[r], dev(dl=1))

    def to_sibling(r):
        lanes = pl.ds(pl.multiple_of(384 * (1 - c), 128), HALF)
        return remote(g_buf.at[r, :, lanes], h_buf.at[r], h_send.at[r], h_recv.at[r], dev(dc=1))

    def act_part(src, dst, half, to, i):
        at = pl.ds(half * (MSG // 2), MSG // 2)
        return remote(a_buf.at[src, at, own], a_buf.at[dst, at, own], a_send.at[i], a_recv.at[i], to)

    def act_whole(i, half):
        src, dst, to = [
            (0, 3, dev(dx=1)),
            (0, 2, dev(dy=1)), (0, 1, dev(dy=-1)),
            (3, 5, dev(dy=1)), (3, 4, dev(dy=-1)),
        ][i]
        return act_part(src, dst, half, to, 2 * i + half)

    def act_half(i):
        src, dst, to = [(2, 6, dev(dy=1)), (1, 6, dev(dy=-1)), (5, 7, dev(dy=1)), (4, 7, dev(dy=-1))][i]
        return act_part(src, dst, i % 2, to, 10 + i)

    def act_over_x(half):
        return act_part(6, 7, half, dev(dx=1), 14 + half)

    def act_sibling(r):
        return remote(
            a_buf.at[r, :, own], a_buf.at[r, :, other], as_send.at[r], as_recv.at[r], dev(dc=1)
        )

    transfers = {
        "direct": direct, "x_lo": to_x_lo, "columns": to_sibling,
        "z_first": lambda r, way: along_z(r, 0, way), "z_second": lambda r, way: along_z(r, 1, way),
        "act": act_whole, "act_half": act_half,
        "act_over_x": act_over_x, "act_core": act_sibling,
    }

    def run(todo):
        for go, name, *which in todo:
            if go:
                transfers[name](*which).start()
            else:
                (direct_in if name == "direct" else transfers[name])(*which).wait_recv()

    pl.semaphore_wait(barrier, len(peers))
    early = [item for item in FIRST if item[1] == "direct"]
    run(early)

    rhs[...] = jnp.zeros_like(rhs)
    acc[...] = jnp.zeros_like(acc)
    for load in loads[:3]:
        load.wait()

    labels = lax.broadcasted_iota(jnp.int32, (128, TOK), 0)
    in_example = (jnp.broadcast_to(segment_buf[...], (128, TOK)) == labels).astype(F32).astype(BF16)
    order_rows = jnp.broadcast_to(order_buf[...].astype(F32), (16, 128)).astype(BF16)
    rows = jnp.dot(order_rows, in_example, preferred_element_type=F32)
    picked = jnp.broadcast_to(rows[0:1, :], (128, TOK)) == labels.astype(F32)
    q = q_buf[...]
    q1 = q.astype(BF16).astype(F32)
    q2 = (q - q1).astype(BF16).astype(F32)
    q3 = q - q1 - q2
    parts = jnp.concatenate([q1, q2, q3, jnp.zeros_like(q)], axis=0).astype(BF16)
    weights = jnp.dot(parts, picked.astype(F32).astype(BF16), preferred_element_type=F32)
    a_buf[0, pl.ds(WIN, MSG - WIN), own] = weights.astype(BF16)
    loads[3].wait()

    run([item for item in FIRST if item not in early and item[1] != "columns"])
    loads[4].wait()
    to_sibling(0).start()

    def load_rhs(r, half):
        at = pl.ds(half * TOK, TOK)

        @pl.when(c == 0)
        def _():
            rhs[at, :] = g_buf[r, :, 0:HALF] if half == 0 else h_buf[r]

        @pl.when(c == 1)
        def _():
            rhs[at, 0:WIN] = g_buf[r, :, SLAB - WIN:SLAB] if half == 0 else h_buf[r, :, HALF - WIN:HALF]

    def add(r, size, at):
        for row in range(0, WIN, size):
            acc[pl.ds(row * K, size * K), :] += product(a_buf.at[r], rhs, row, size, at)

    def step(n, _):
        for i, (todo, _, _) in enumerate(STEPS[:-1]):
            if todo:
                pl.when(n == i)(lambda todo=todo: run(todo))
        r = sum(jnp.where(n == i, r, 0) for i, (_, r, _) in enumerate(STEPS[:-1]))
        mode = sum(jnp.where(n == i, mode, 0) for i, (_, _, mode) in enumerate(STEPS[:-1]))

        @pl.when(mode != 1)
        def _():
            load_rhs(r, 0)

        @pl.when(mode != 0)
        def _():
            load_rhs(r, 1)

        @pl.when(mode == 2)
        def _():
            add(r, WIDE, pl.ds(0, 2 * TOK))

        @pl.when(mode != 2)
        def _():
            add(r, BLOCK, pl.ds(pl.multiple_of(mode * TOK, TOK), TOK))

        return 0

    lax.fori_loop(0, len(STEPS) - 1, step, 0)
    todo, r, mode = STEPS[-1]
    run(todo)
    if mode != 1:
        load_rhs(r, 0)
    if mode != 0:
        load_rhs(r, 1)
    a_last[...] = a_buf[r]

    for todo in [FIRST] + [step[0] for step in STEPS]:
        for go, name, *which in todo:
            if go:
                transfers[name](*which).wait_send()


def local(act, grad_out, q_cols, example_order, segment):
    dma = pltpu.SemaphoreType.DMA
    hbm = [
        pltpu.with_memory_space_constraint(v, pltpu.HBM)
        for v in (act.T, grad_out, q_cols.T, example_order[None, :], segment[None, :])
    ]
    vmem = pl.BlockSpec(memory_space=pltpu.VMEM)
    parts = pl.pallas_call(
        kernel,
        out_shape=[
            jax.ShapeDtypeStruct((WIN * K, HALF), F32),
            jax.ShapeDtypeStruct((MSG, 2 * TOK), BF16),
            jax.ShapeDtypeStruct((2 * TOK, HALF), BF16),
        ],
        in_specs=[pl.BlockSpec(memory_space=pltpu.HBM)] * 5,
        out_specs=[vmem] * 3,
        scratch_shapes=[
            pltpu.VMEM((GROUPS, MSG, 2 * TOK), BF16),
            pltpu.VMEM((GROUPS, TOK, SLAB), BF16),
            pltpu.VMEM((GROUPS, TOK, HALF), BF16),
            pltpu.VMEM((K, 128), F32),
            pltpu.VMEM((1, 128), jnp.int32),
            pltpu.VMEM((1, TOK), jnp.int32),
            dma((5,)),
            dma((16,)), dma((16,)), dma((GROUPS,)), dma((GROUPS,)),
            dma((GROUPS,)), dma((GROUPS,)), dma((GROUPS, 4)), dma((GROUPS, 4)),
            dma((GROUPS,)), dma((GROUPS,)), dma((GROUPS,)), dma((GROUPS,)),
        ],
        compiler_params=pltpu.CompilerParams(
            collective_id=1, has_side_effects=True, vmem_limit_bytes=24 * 1024 * 1024
        ),
    )(*hbm)
    return pl.pallas_call(
        finish,
        out_shape=jax.ShapeDtypeStruct((WIN, K, WIN), BF16),
        in_specs=[vmem] * 3,
        out_specs=pl.BlockSpec(memory_space=pltpu.HBM),
        scratch_shapes=[pltpu.VMEM((WIN, K, WIN), BF16), dma((WIN // BLOCK,))],
        compiler_params=pltpu.CompilerParams(vmem_limit_bytes=16 * 1024 * 1024),
    )(*[pltpu.with_memory_space_constraint(v, pltpu.VMEM) for v in parts])


def solution(mesh):
    in_specs = (P("ex", "tp"), P("ex", None), P(), P(), P("ex"))
    out_specs = P("tp", None, "ex")
    return jax.shard_map(local, mesh=mesh, in_specs=in_specs, out_specs=out_specs, check_vma=False)
```

```python
import jax
import jax.numpy as jnp
from jax import lax
from jax.experimental import pallas as pl
from jax.experimental.pallas import tpu as pltpu
from jax.sharding import PartitionSpec as P

MESH = pl.DeviceIdType.MESH
BF16, F32 = jnp.bfloat16, jnp.float32
NX, NY, NZ = 2, 4, 8
TOK = 256
WIN = 448
SLAB = 896
HALF = 512
MSG = 480
K = 8
FINE = 64
BLOCK = 112
WIDE = 224
SOURCES = ((0, 0), (0, 1), (0, 3), (1, 0), (1, 1), (1, 3), (0, 2), (1, 2))
GROUPS = len(SOURCES)
WHOLE = (3,)
SPLIT = (2, 4, 7)
GO, GET = True, False
FIRST = (
    (GO, 'act_core', 0),
    (GO, 'columns', 0),
    (GO, 'direct', 4),
    (GO, 'direct', 2),
    (GO, 'act', 0, 0),
    (GO, 'act', 0, 1),
    (GO, 'direct', 7),
    (GO, 'direct', 5),
    (GO, 'act', 1, 0),
    (GO, 'act', 1, 1),
    (GO, 'direct', 1),
    (GO, 'act', 2, 0),
    (GO, 'act', 2, 1),
)
STEPS = (
    ((), 0, 0),
    ((
        (GET, 'act_core', 0),
        (GET, 'columns', 0),
    ), 0, 1),
    ((
        (GET, 'direct', 2),
        (GO, 'z_first', 2, 1),
        (GO, 'z_first', 2, 0),
        (GET, 'direct', 4),
        (GO, 'z_first', 4, 0),
        (GO, 'z_first', 4, 1),
        (GO, 'direct', 3),
        (GO, 'direct', 6),
        (GET, 'z_first', 2, 1),
        (GET, 'z_first', 2, 0),
        (GO, 'z_second', 2, 0),
        (GO, 'z_second', 2, 1),
        (GET, 'direct', 1),
        (GO, 'z_first', 1, 0),
        (GO, 'z_first', 1, 1),
        (GET, 'z_first', 4, 0),
        (GET, 'z_first', 4, 1),
        (GO, 'z_second', 4, 1),
        (GO, 'z_second', 4, 0),
        (GET, 'z_second', 2, 0),
        (GET, 'z_second', 2, 1),
        (GO, 'x_lo', 2),
        (GET, 'act', 0, 0),
        (GET, 'act', 0, 1),
        (GO, 'act_core', 3),
        (GO, 'act', 4, 0),
        (GO, 'act', 4, 1),
        (GET, 'direct', 7),
        (GO, 'act', 3, 0),
        (GO, 'act', 3, 1),
        (GO, 'z_first', 7, 0),
        (GO, 'z_first', 7, 1),
        (GET, 'act_core', 3),
        (GET, 'z_first', 1, 0),
        (GET, 'z_first', 1, 1),
        (GO, 'z_second', 1, 1),
        (GO, 'z_second', 1, 0),
        (GET, 'z_second', 4, 1),
        (GET, 'z_second', 4, 0),
        (GO, 'x_lo', 4),
        (GET, 'act', 1, 0),
        (GET, 'act', 1, 1),
        (GO, 'act_core', 2),
        (GET, 'act', 2, 0),
        (GET, 'act', 2, 1),
        (GO, 'act_core', 1),
        (GO, 'act_half', 0),
        (GO, 'act_half', 1),
        (GET, 'direct', 5),
        (GO, 'z_first', 5, 0),
        (GO, 'z_first', 5, 1),
        (GET, 'z_first', 7, 0),
        (GET, 'z_first', 7, 1),
        (GO, 'z_second', 7, 1),
        (GO, 'z_second', 7, 0),
        (GET, 'act_core', 2),
        (GET, 'act_core', 1),
        (GET, 'z_second', 1, 1),
        (GET, 'z_second', 1, 0),
        (GO, 'columns', 1),
    ), 1, 0),
    ((
        (GET, 'x_lo', 2),
        (GO, 'columns', 2),
        (GET, 'direct', 6),
        (GO, 'z_first', 6, 0),
        (GO, 'z_first', 6, 1),
    ), 2, 0),
    ((
        (GET, 'columns', 1),
        (GET, 'z_first', 5, 0),
        (GET, 'z_first', 5, 1),
        (GO, 'z_second', 5, 0),
        (GO, 'z_second', 5, 1),
    ), 1, 1),
    ((
        (GET, 'columns', 2),
        (GET, 'z_second', 7, 1),
        (GET, 'z_second', 7, 0),
        (GO, 'x_lo', 7),
    ), 2, 1),
    ((
        (GET, 'z_first', 6, 0),
        (GET, 'z_first', 6, 1),
        (GO, 'z_second', 6, 1),
        (GO, 'z_second', 6, 0),
        (GET, 'act', 4, 0),
        (GET, 'act', 4, 1),
        (GO, 'act_core', 4),
        (GET, 'act', 3, 0),
        (GET, 'act', 3, 1),
        (GO, 'act_core', 5),
        (GO, 'act_half', 3),
        (GO, 'act_half', 2),
        (GET, 'x_lo', 4),
        (GO, 'columns', 4),
    ), 4, 0),
    ((
        (GET, 'z_second', 5, 0),
        (GET, 'z_second', 5, 1),
        (GO, 'columns', 5),
    ), 5, 0),
    ((
        (GET, 'act_core', 4),
        (GET, 'act_core', 5),
        (GET, 'direct', 3),
        (GO, 'columns', 3),
        (GET, 'columns', 4),
    ), 4, 1),
    ((
        (GET, 'z_second', 6, 1),
        (GET, 'z_second', 6, 0),
        (GO, 'columns', 6),
        (GET, 'act_half', 0),
        (GET, 'act_half', 1),
        (GO, 'act_core', 6),
        (GET, 'columns', 5),
    ), 5, 1),
    ((
        (GET, 'columns', 3),
        (GET, 'x_lo', 7),
        (GO, 'columns', 7),
    ), 3, 2),
    ((
        (GET, 'act_half', 3),
        (GET, 'act_half', 2),
        (GO, 'act_core', 7),
        (GET, 'columns', 6),
        (GET, 'act_core', 6),
        (GET, 'columns', 7),
    ), 6, 2),
    ((
        (GET, 'act_core', 7),
    ), 7, 2),
)

def product(a, rhs, row, size, at):
    w = a[WIN:WIN + 32, at].astype(F32)
    w = w[0:8] + w[8:16] + w[16:24]
    left = a[pl.ds(row, size), at].astype(F32)
    left = (left[:, None, :] * w[None, :, :]).astype(BF16).reshape(size * K, at.size)
    return jnp.dot(left, rhs[at, :], preferred_element_type=F32)


def finish(acc, a_last, rhs, out, stage, sem):
    at = (pl.ds(0, TOK), pl.ds(TOK, TOK), pl.ds(0, 2 * TOK))[STEPS[-1][2]]
    copies = []
    for i, row in enumerate(range(0, WIN, FINE)):
        total = acc[pl.ds(row * K, FINE * K), :] + product(a_last, rhs, row, FINE, at)
        stage[pl.ds(row, FINE)] = total[:, 0:WIN].reshape(FINE, K, WIN).astype(BF16)
        rows = pl.ds(row, FINE)
        copies.append(pltpu.make_async_copy(stage.at[rows], out.at[rows], sem.at[i]))
        copies[-1].start()
    for copy in copies:
        copy.wait()


def kernel(
    act, grad, q_cols, order, segment, acc, a_last, rhs,
    a_buf, g_buf, h_buf, q_buf, order_buf, segment_buf, local_sem,
    a_send, a_recv, as_send, as_recv, d_send, d_recv, z_send, z_recv, x_send, x_recv, h_send, h_recv,
):
    e, t = lax.axis_index("ex"), lax.axis_index("tp")
    xh, y, c = e // 8, (e // 2) % 4, e % 2
    z, xl = t // 2, t % 2
    share = z % 4

    def dev(dx=0, dy=0, dz=0, dc=0, dl=0):
        return (
            ((xh + dx) % NX) * 8 + ((y + dy + NY) % NY) * 2 + (c + dc) % 2,
            ((z + dz + NZ) % NZ) * 2 + (xl + dl) % 2,
        )

    def remote(src, dst, send, recv, to):
        return pltpu.make_async_remote_copy(
            src_ref=src, dst_ref=dst, send_sem=send, recv_sem=recv,
            device_id=to, device_id_type=MESH,
        )

    barrier = pltpu.get_barrier_semaphore()
    peers = [dev(dx, dy, dl=dx) for dx, dy in SOURCES[1:]]
    peers += [dev(dx=1), dev(dl=1), dev(dz=1), dev(dz=-1), dev(dc=1)]
    for peer in peers:
        pl.semaphore_signal(barrier, inc=1, device_id=peer, device_id_type=MESH)

    own = pl.ds(0, TOK)
    other = pl.ds(TOK, TOK)
    slab = pl.multiple_of(SLAB * (4 * xh + y), 128)
    loads = [
        pltpu.make_async_copy(src, dst, local_sem.at[i])
        for i, (src, dst) in enumerate([
            (order, order_buf), (segment, segment_buf), (q_cols, q_buf),
            (act, a_buf.at[0, pl.ds(0, WIN), own]),
            (grad.at[:, pl.ds(slab, SLAB)], g_buf.at[0]),
        ])
    ]
    for load in loads:
        load.start()
    def quarter(r, q, side, half=None):
        if r in WHOLE:
            return pl.ds(0, TOK)
        rows = TOK // 8 if r in SPLIT else TOK // 4
        at = q * rows + (side * (TOK // 2) if r in SPLIT else 0)
        if half is not None:
            rows = rows // 2
            at = at + half * rows
        return pl.ds(pl.multiple_of(at, rows), rows)

    def direct(r):
        dx, dy = SOURCES[r]
        to_x, to_y = (xh + dx) % NX, (y - dy + NY) % NY
        lanes = pl.ds(pl.multiple_of(SLAB * (4 * to_x + to_y), 128), SLAB)
        rows = quarter(r, share, (xl + dx) % 2)
        return remote(
            grad.at[rows, lanes], g_buf.at[r, rows, :], d_send.at[r], d_recv.at[r], dev(dx, -dy, dl=dx)
        )

    def direct_in(r):
        part = g_buf.at[r, quarter(r, share, xl), :]
        return remote(part, part, d_send.at[r], d_recv.at[r], dev(dc=1))

    def along_z(r, hop, way):
        if hop == 0:
            at = quarter(r, share, xl)
        else:
            at = quarter(r, (share + (3 if way == 0 else 1)) % 4, xl, way)
        part = g_buf.at[r, at, :]
        i = hop * 2 + way
        return remote(part, part, z_send.at[r, i], z_recv.at[r, i], dev(dz=1 if way == 0 else -1))

    def to_x_lo(r):
        half = TOK // 2
        part = g_buf.at[r, pl.ds(pl.multiple_of(xl * half, half), half), :]
        return remote(part, part, x_send.at[r], x_recv.at[r], dev(dl=1))

    def to_sibling(r):
        lanes = pl.ds(pl.multiple_of(384 * (1 - c), 128), HALF)
        return remote(g_buf.at[r, :, lanes], h_buf.at[r], h_send.at[r], h_recv.at[r], dev(dc=1))

    def act_part(src, dst, half, to, i):
        at = pl.ds(half * (MSG // 2), MSG // 2)
        return remote(a_buf.at[src, at, own], a_buf.at[dst, at, own], a_send.at[i], a_recv.at[i], to)

    def act_whole(i, half):
        src, dst, to = [
            (0, 3, dev(dx=1)),
            (0, 2, dev(dy=1)), (0, 1, dev(dy=-1)),
            (3, 5, dev(dy=1)), (3, 4, dev(dy=-1)),
        ][i]
        return act_part(src, dst, half, to, 2 * i + half)

    def act_half(i):
        src, dst, to = [(2, 6, dev(dy=1)), (1, 6, dev(dy=-1)), (5, 7, dev(dy=1)), (4, 7, dev(dy=-1))][i]
        return act_part(src, dst, i % 2, to, 10 + i)

    def act_over_x(half):
        return act_part(6, 7, half, dev(dx=1), 14 + half)

    def act_sibling(r):
        return remote(
            a_buf.at[r, :, own], a_buf.at[r, :, other], as_send.at[r], as_recv.at[r], dev(dc=1)
        )

    transfers = {
        "direct": direct, "x_lo": to_x_lo, "columns": to_sibling,
        "z_first": lambda r, way: along_z(r, 0, way), "z_second": lambda r, way: along_z(r, 1, way),
        "act": act_whole, "act_half": act_half,
        "act_over_x": act_over_x, "act_core": act_sibling,
    }

    def run(todo):
        for go, name, *which in todo:
            if go:
                transfers[name](*which).start()
            else:
                (direct_in if name == "direct" else transfers[name])(*which).wait_recv()

    pl.semaphore_wait(barrier, len(peers))
    early = [item for item in FIRST if item[1] == "direct"]
    run(early)

    rhs[...] = jnp.zeros_like(rhs)
    acc[...] = jnp.zeros_like(acc)
    for load in loads[:3]:
        load.wait()

    labels = lax.broadcasted_iota(jnp.int32, (128, TOK), 0)
    in_example = (jnp.broadcast_to(segment_buf[...], (128, TOK)) == labels).astype(F32).astype(BF16)
    order_rows = jnp.broadcast_to(order_buf[...].astype(F32), (16, 128)).astype(BF16)
    rows = jnp.dot(order_rows, in_example, preferred_element_type=F32)
    picked = jnp.broadcast_to(rows[0:1, :], (128, TOK)) == labels.astype(F32)
    q = q_buf[...]
    q1 = q.astype(BF16).astype(F32)
    q2 = (q - q1).astype(BF16).astype(F32)
    q3 = q - q1 - q2
    parts = jnp.concatenate([q1, q2, q3, jnp.zeros_like(q)], axis=0).astype(BF16)
    weights = jnp.dot(parts, picked.astype(F32).astype(BF16), preferred_element_type=F32)
    a_buf[0, pl.ds(WIN, MSG - WIN), own] = weights.astype(BF16)
    loads[3].wait()

    run([item for item in FIRST if item not in early and item[1] != "columns"])
    loads[4].wait()
    to_sibling(0).start()

    def load_rhs(r, half):
        at = pl.ds(half * TOK, TOK)

        @pl.when(c == 0)
        def _():
            rhs[at, :] = g_buf[r, :, 0:HALF] if half == 0 else h_buf[r]

        @pl.when(c == 1)
        def _():
            rhs[at, 0:WIN] = g_buf[r, :, SLAB - WIN:SLAB] if half == 0 else h_buf[r, :, HALF - WIN:HALF]

    def add(r, size, at):
        for row in range(0, WIN, size):
            acc[pl.ds(row * K, size * K), :] += product(a_buf.at[r], rhs, row, size, at)

    def step(n, _):
        for i, (todo, _, _) in enumerate(STEPS[:-1]):
            if todo:
                pl.when(n == i)(lambda todo=todo: run(todo))
        r = sum(jnp.where(n == i, r, 0) for i, (_, r, _) in enumerate(STEPS[:-1]))
        mode = sum(jnp.where(n == i, mode, 0) for i, (_, _, mode) in enumerate(STEPS[:-1]))

        @pl.when(mode != 1)
        def _():
            load_rhs(r, 0)

        @pl.when(mode != 0)
        def _():
            load_rhs(r, 1)

        @pl.when(mode == 2)
        def _():
            add(r, WIDE, pl.ds(0, 2 * TOK))

        @pl.when(mode != 2)
        def _():
            add(r, BLOCK, pl.ds(pl.multiple_of(mode * TOK, TOK), TOK))

        return 0

    lax.fori_loop(0, len(STEPS) - 1, step, 0)
    todo, r, mode = STEPS[-1]
    run(todo)
    if mode != 1:
        load_rhs(r, 0)
    if mode != 0:
        load_rhs(r, 1)
    a_last[...] = a_buf[r]

    for todo in [FIRST] + [step[0] for step in STEPS]:
        for go, name, *which in todo:
            if go:
                transfers[name](*which).wait_send()


def local(act, grad_out, q_cols, example_order, segment):
    dma = pltpu.SemaphoreType.DMA
    hbm = [
        pltpu.with_memory_space_constraint(v, pltpu.HBM)
        for v in (act.T, grad_out, q_cols.T, example_order[None, :], segment[None, :])
    ]
    vmem = pl.BlockSpec(memory_space=pltpu.VMEM)
    parts = pl.pallas_call(
        kernel,
        out_shape=[
            jax.ShapeDtypeStruct((WIN * K, HALF), F32),
            jax.ShapeDtypeStruct((MSG, 2 * TOK), BF16),
            jax.ShapeDtypeStruct((2 * TOK, HALF), BF16),
        ],
        in_specs=[pl.BlockSpec(memory_space=pltpu.HBM)] * 5,
        out_specs=[vmem] * 3,
        scratch_shapes=[
            pltpu.VMEM((GROUPS, MSG, 2 * TOK), BF16),
            pltpu.VMEM((GROUPS, TOK, SLAB), BF16),
            pltpu.VMEM((GROUPS, TOK, HALF), BF16),
            pltpu.VMEM((K, 128), F32),
            pltpu.VMEM((1, 128), jnp.int32),
            pltpu.VMEM((1, TOK), jnp.int32),
            dma((5,)),
            dma((16,)), dma((16,)), dma((GROUPS,)), dma((GROUPS,)),
            dma((GROUPS,)), dma((GROUPS,)), dma((GROUPS, 4)), dma((GROUPS, 4)),
            dma((GROUPS,)), dma((GROUPS,)), dma((GROUPS,)), dma((GROUPS,)),
        ],
        compiler_params=pltpu.CompilerParams(
            collective_id=1, has_side_effects=True, vmem_limit_bytes=24 * 1024 * 1024
        ),
    )(*hbm)
    return pl.pallas_call(
        finish,
        out_shape=jax.ShapeDtypeStruct((WIN, K, WIN), BF16),
        in_specs=[vmem] * 3,
        out_specs=pl.BlockSpec(memory_space=pltpu.HBM),
        scratch_shapes=[pltpu.VMEM((WIN, K, WIN), BF16), dma((WIN // FINE,))],
        compiler_params=pltpu.CompilerParams(vmem_limit_bytes=16 * 1024 * 1024),
    )(*[pltpu.with_memory_space_constraint(v, pltpu.VMEM) for v in parts])


def solution(mesh):
    in_specs = (P("ex", "tp"), P("ex", None), P(), P(), P("ex"))
    out_specs = P("tp", None, "ex")
    return jax.shard_map(local, mesh=mesh, in_specs=in_specs, out_specs=out_specs, check_vma=False)
```

```python
import jax
import jax.numpy as jnp
from jax import lax
from jax.experimental import pallas as pl
from jax.experimental.pallas import tpu as pltpu
from jax.sharding import PartitionSpec as P

MESH = pl.DeviceIdType.MESH
BF16, F32 = jnp.bfloat16, jnp.float32
NX, NY, NZ = 2, 4, 8
TOK = 256
WIN = 448
SLAB = 896
HALF = 512
MSG = 480
K = 8
FINE = 64
BLOCK = 224
WIDE = 448
SOURCES = ((0, 0), (0, 1), (0, 3), (1, 0), (1, 1), (1, 3), (0, 2), (1, 2))
GROUPS = len(SOURCES)
WHOLE = (3,)
SPLIT = (2, 4, 7)
GO, GET = True, False
FIRST = (
    (GO, 'act_core', 0),
    (GO, 'columns', 0),
    (GO, 'direct', 4),
    (GO, 'direct', 2),
    (GO, 'act', 0, 0),
    (GO, 'act', 0, 1),
    (GO, 'direct', 7),
    (GO, 'direct', 5),
    (GO, 'act', 1, 0),
    (GO, 'act', 1, 1),
    (GO, 'direct', 1),
    (GO, 'act', 2, 0),
    (GO, 'act', 2, 1),
)
STEPS = (
    ((), 0, 0),
    ((
        (GET, 'act_core', 0),
        (GET, 'columns', 0),
    ), 0, 1),
    ((
        (GET, 'direct', 2),
        (GO, 'z_first', 2, 1),
        (GO, 'z_first', 2, 0),
        (GET, 'direct', 4),
        (GO, 'z_first', 4, 0),
        (GO, 'z_first', 4, 1),
        (GO, 'direct', 3),
        (GO, 'direct', 6),
        (GET, 'z_first', 2, 1),
        (GET, 'z_first', 2, 0),
        (GO, 'z_second', 2, 0),
        (GO, 'z_second', 2, 1),
        (GET, 'direct', 1),
        (GO, 'z_first', 1, 0),
        (GO, 'z_first', 1, 1),
        (GET, 'z_first', 4, 0),
        (GET, 'z_first', 4, 1),
        (GO, 'z_second', 4, 1),
        (GO, 'z_second', 4, 0),
        (GET, 'z_second', 2, 0),
        (GET, 'z_second', 2, 1),
        (GO, 'x_lo', 2),
        (GET, 'act', 0, 0),
        (GET, 'act', 0, 1),
        (GO, 'act_core', 3),
        (GO, 'act', 4, 0),
        (GO, 'act', 4, 1),
        (GET, 'direct', 7),
        (GO, 'act', 3, 0),
        (GO, 'act', 3, 1),
        (GO, 'z_first', 7, 0),
        (GO, 'z_first', 7, 1),
        (GET, 'act_core', 3),
        (GET, 'z_first', 1, 0),
        (GET, 'z_first', 1, 1),
        (GO, 'z_second', 1, 1),
        (GO, 'z_second', 1, 0),
        (GET, 'z_second', 4, 1),
        (GET, 'z_second', 4, 0),
        (GO, 'x_lo', 4),
        (GET, 'act', 1, 0),
        (GET, 'act', 1, 1),
        (GO, 'act_core', 2),
        (GET, 'act', 2, 0),
        (GET, 'act', 2, 1),
        (GO, 'act_core', 1),
        (GO, 'act_half', 0),
        (GO, 'act_half', 1),
        (GET, 'direct', 5),
        (GO, 'z_first', 5, 0),
        (GO, 'z_first', 5, 1),
        (GET, 'z_first', 7, 0),
        (GET, 'z_first', 7, 1),
        (GO, 'z_second', 7, 1),
        (GO, 'z_second', 7, 0),
        (GET, 'act_core', 2),
        (GET, 'act_core', 1),
        (GET, 'z_second', 1, 1),
        (GET, 'z_second', 1, 0),
        (GO, 'columns', 1),
    ), 1, 0),
    ((
        (GET, 'x_lo', 2),
        (GO, 'columns', 2),
        (GET, 'direct', 6),
        (GO, 'z_first', 6, 0),
        (GO, 'z_first', 6, 1),
    ), 2, 0),
    ((
        (GET, 'columns', 1),
        (GET, 'z_first', 5, 0),
        (GET, 'z_first', 5, 1),
        (GO, 'z_second', 5, 0),
        (GO, 'z_second', 5, 1),
    ), 1, 1),
    ((
        (GET, 'columns', 2),
        (GET, 'z_second', 7, 1),
        (GET, 'z_second', 7, 0),
        (GO, 'x_lo', 7),
    ), 2, 1),
    ((
        (GET, 'z_first', 6, 0),
        (GET, 'z_first', 6, 1),
        (GO, 'z_second', 6, 1),
        (GO, 'z_second', 6, 0),
        (GET, 'act', 4, 0),
        (GET, 'act', 4, 1),
        (GO, 'act_core', 4),
        (GET, 'act', 3, 0),
        (GET, 'act', 3, 1),
        (GO, 'act_core', 5),
        (GO, 'act_half', 3),
        (GO, 'act_half', 2),
        (GET, 'x_lo', 4),
        (GO, 'columns', 4),
    ), 4, 0),
    ((
        (GET, 'z_second', 5, 0),
        (GET, 'z_second', 5, 1),
        (GO, 'columns', 5),
    ), 5, 0),
    ((
        (GET, 'act_core', 4),
        (GET, 'act_core', 5),
        (GET, 'direct', 3),
        (GO, 'columns', 3),
        (GET, 'columns', 4),
    ), 4, 1),
    ((
        (GET, 'z_second', 6, 1),
        (GET, 'z_second', 6, 0),
        (GO, 'columns', 6),
        (GET, 'act_half', 0),
        (GET, 'act_half', 1),
        (GO, 'act_core', 6),
        (GET, 'columns', 5),
    ), 5, 1),
    ((
        (GET, 'columns', 3),
        (GET, 'x_lo', 7),
        (GO, 'columns', 7),
    ), 3, 2),
    ((
        (GET, 'act_half', 3),
        (GET, 'act_half', 2),
        (GO, 'act_core', 7),
        (GET, 'columns', 6),
        (GET, 'act_core', 6),
        (GET, 'columns', 7),
    ), 6, 2),
    ((
        (GET, 'act_core', 7),
    ), 7, 2),
)

def product(a, rhs, row, size, at):
    w = a[WIN:WIN + 32, at].astype(F32)
    w = w[0:8] + w[8:16] + w[16:24]
    left = a[pl.ds(row, size), at].astype(F32)
    left = (left[:, None, :] * w[None, :, :]).astype(BF16).reshape(size * K, at.size)
    return jnp.dot(left, rhs[at, :], preferred_element_type=F32)


def finish(acc, a_last, rhs, out, stage, sem):
    at = (pl.ds(0, TOK), pl.ds(TOK, TOK), pl.ds(0, 2 * TOK))[STEPS[-1][2]]
    copies = []
    for i, row in enumerate(range(0, WIN, FINE)):
        total = acc[pl.ds(row * K, FINE * K), :] + product(a_last, rhs, row, FINE, at)
        stage[pl.ds(row, FINE)] = total[:, 0:WIN].reshape(FINE, K, WIN).astype(BF16)
        rows = pl.ds(row, FINE)
        copies.append(pltpu.make_async_copy(stage.at[rows], out.at[rows], sem.at[i]))
        copies[-1].start()
    for copy in copies:
        copy.wait()


def kernel(
    act, grad, q_cols, order, segment, acc, a_last, rhs,
    a_buf, g_buf, h_buf, q_buf, order_buf, segment_buf, local_sem,
    a_send, a_recv, as_send, as_recv, d_send, d_recv, z_send, z_recv, x_send, x_recv, h_send, h_recv,
):
    e, t = lax.axis_index("ex"), lax.axis_index("tp")
    xh, y, c = e // 8, (e // 2) % 4, e % 2
    z, xl = t // 2, t % 2
    share = z % 4

    def dev(dx=0, dy=0, dz=0, dc=0, dl=0):
        return (
            ((xh + dx) % NX) * 8 + ((y + dy + NY) % NY) * 2 + (c + dc) % 2,
            ((z + dz + NZ) % NZ) * 2 + (xl + dl) % 2,
        )

    def remote(src, dst, send, recv, to):
        return pltpu.make_async_remote_copy(
            src_ref=src, dst_ref=dst, send_sem=send, recv_sem=recv,
            device_id=to, device_id_type=MESH,
        )

    barrier = pltpu.get_barrier_semaphore()
    peers = [dev(dx, dy, dl=dx) for dx, dy in SOURCES[1:]]
    peers += [dev(dx=1), dev(dl=1), dev(dz=1), dev(dz=-1), dev(dc=1)]
    for peer in peers:
        pl.semaphore_signal(barrier, inc=1, device_id=peer, device_id_type=MESH)

    own = pl.ds(0, TOK)
    other = pl.ds(TOK, TOK)
    slab = pl.multiple_of(SLAB * (4 * xh + y), 128)
    loads = [
        pltpu.make_async_copy(src, dst, local_sem.at[i])
        for i, (src, dst) in enumerate([
            (order, order_buf), (segment, segment_buf), (q_cols, q_buf),
            (act, a_buf.at[0, pl.ds(0, WIN), own]),
            (grad.at[:, pl.ds(slab, SLAB)], g_buf.at[0]),
        ])
    ]
    for load in loads:
        load.start()
    def quarter(r, q, side, half=None):
        if r in WHOLE:
            return pl.ds(0, TOK)
        rows = TOK // 8 if r in SPLIT else TOK // 4
        at = q * rows + (side * (TOK // 2) if r in SPLIT else 0)
        if half is not None:
            rows = rows // 2
            at = at + half * rows
        return pl.ds(pl.multiple_of(at, rows), rows)

    def direct(r):
        dx, dy = SOURCES[r]
        to_x, to_y = (xh + dx) % NX, (y - dy + NY) % NY
        lanes = pl.ds(pl.multiple_of(SLAB * (4 * to_x + to_y), 128), SLAB)
        rows = quarter(r, share, (xl + dx) % 2)
        return remote(
            grad.at[rows, lanes], g_buf.at[r, rows, :], d_send.at[r], d_recv.at[r], dev(dx, -dy, dl=dx)
        )

    def direct_in(r):
        part = g_buf.at[r, quarter(r, share, xl), :]
        return remote(part, part, d_send.at[r], d_recv.at[r], dev(dc=1))

    def along_z(r, hop, way):
        if hop == 0:
            at = quarter(r, share, xl)
        else:
            at = quarter(r, (share + (3 if way == 0 else 1)) % 4, xl, way)
        part = g_buf.at[r, at, :]
        i = hop * 2 + way
        return remote(part, part, z_send.at[r, i], z_recv.at[r, i], dev(dz=1 if way == 0 else -1))

    def to_x_lo(r):
        half = TOK // 2
        part = g_buf.at[r, pl.ds(pl.multiple_of(xl * half, half), half), :]
        return remote(part, part, x_send.at[r], x_recv.at[r], dev(dl=1))

    def to_sibling(r):
        lanes = pl.ds(pl.multiple_of(384 * (1 - c), 128), HALF)
        return remote(g_buf.at[r, :, lanes], h_buf.at[r], h_send.at[r], h_recv.at[r], dev(dc=1))

    def act_part(src, dst, half, to, i):
        at = pl.ds(half * (MSG // 2), MSG // 2)
        return remote(a_buf.at[src, at, own], a_buf.at[dst, at, own], a_send.at[i], a_recv.at[i], to)

    def act_whole(i, half):
        src, dst, to = [
            (0, 3, dev(dx=1)),
            (0, 2, dev(dy=1)), (0, 1, dev(dy=-1)),
            (3, 5, dev(dy=1)), (3, 4, dev(dy=-1)),
        ][i]
        return act_part(src, dst, half, to, 2 * i + half)

    def act_half(i):
        src, dst, to = [(2, 6, dev(dy=1)), (1, 6, dev(dy=-1)), (5, 7, dev(dy=1)), (4, 7, dev(dy=-1))][i]
        return act_part(src, dst, i % 2, to, 10 + i)

    def act_over_x(half):
        return act_part(6, 7, half, dev(dx=1), 14 + half)

    def act_sibling(r):
        return remote(
            a_buf.at[r, :, own], a_buf.at[r, :, other], as_send.at[r], as_recv.at[r], dev(dc=1)
        )

    transfers = {
        "direct": direct, "x_lo": to_x_lo, "columns": to_sibling,
        "z_first": lambda r, way: along_z(r, 0, way), "z_second": lambda r, way: along_z(r, 1, way),
        "act": act_whole, "act_half": act_half,
        "act_over_x": act_over_x, "act_core": act_sibling,
    }

    def run(todo):
        for go, name, *which in todo:
            if go:
                transfers[name](*which).start()
            else:
                (direct_in if name == "direct" else transfers[name])(*which).wait_recv()

    pl.semaphore_wait(barrier, len(peers))
    early = [item for item in FIRST if item[1] == "direct"]
    run(early)

    rhs[...] = jnp.zeros_like(rhs)
    acc[...] = jnp.zeros_like(acc)
    for load in loads[:3]:
        load.wait()

    labels = lax.broadcasted_iota(jnp.int32, (128, TOK), 0)
    in_example = (jnp.broadcast_to(segment_buf[...], (128, TOK)) == labels).astype(F32).astype(BF16)
    order_rows = jnp.broadcast_to(order_buf[...].astype(F32), (16, 128)).astype(BF16)
    rows = jnp.dot(order_rows, in_example, preferred_element_type=F32)
    picked = jnp.broadcast_to(rows[0:1, :], (128, TOK)) == labels.astype(F32)
    q = q_buf[...]
    q1 = q.astype(BF16).astype(F32)
    q2 = (q - q1).astype(BF16).astype(F32)
    q3 = q - q1 - q2
    parts = jnp.concatenate([q1, q2, q3, jnp.zeros_like(q)], axis=0).astype(BF16)
    weights = jnp.dot(parts, picked.astype(F32).astype(BF16), preferred_element_type=F32)
    a_buf[0, pl.ds(WIN, MSG - WIN), own] = weights.astype(BF16)
    loads[3].wait()

    run([item for item in FIRST if item not in early and item[1] != "columns"])
    loads[4].wait()
    to_sibling(0).start()

    def load_rhs(r, half):
        at = pl.ds(half * TOK, TOK)

        @pl.when(c == 0)
        def _():
            rhs[at, :] = g_buf[r, :, 0:HALF] if half == 0 else h_buf[r]

        @pl.when(c == 1)
        def _():
            rhs[at, 0:WIN] = g_buf[r, :, SLAB - WIN:SLAB] if half == 0 else h_buf[r, :, HALF - WIN:HALF]

    def add(r, size, at):
        for row in range(0, WIN, size):
            acc[pl.ds(row * K, size * K), :] += product(a_buf.at[r], rhs, row, size, at)

    def step(n, _):
        for i, (todo, _, _) in enumerate(STEPS[:-1]):
            if todo:
                pl.when(n == i)(lambda todo=todo: run(todo))
        r = sum(jnp.where(n == i, r, 0) for i, (_, r, _) in enumerate(STEPS[:-1]))
        mode = sum(jnp.where(n == i, mode, 0) for i, (_, _, mode) in enumerate(STEPS[:-1]))

        @pl.when(mode != 1)
        def _():
            load_rhs(r, 0)

        @pl.when(mode != 0)
        def _():
            load_rhs(r, 1)

        @pl.when(mode == 2)
        def _():
            add(r, WIDE, pl.ds(0, 2 * TOK))

        @pl.when(mode != 2)
        def _():
            add(r, BLOCK, pl.ds(pl.multiple_of(mode * TOK, TOK), TOK))

        return 0

    lax.fori_loop(0, len(STEPS) - 1, step, 0)
    todo, r, mode = STEPS[-1]
    run(todo)
    if mode != 1:
        load_rhs(r, 0)
    if mode != 0:
        load_rhs(r, 1)
    a_last[...] = a_buf[r]

    for todo in [FIRST] + [step[0] for step in STEPS]:
        for go, name, *which in todo:
            if go:
                transfers[name](*which).wait_send()


def local(act, grad_out, q_cols, example_order, segment):
    dma = pltpu.SemaphoreType.DMA
    hbm = [
        pltpu.with_memory_space_constraint(v, pltpu.HBM)
        for v in (act.T, grad_out, q_cols.T, example_order[None, :], segment[None, :])
    ]
    vmem = pl.BlockSpec(memory_space=pltpu.VMEM)
    parts = pl.pallas_call(
        kernel,
        out_shape=[
            jax.ShapeDtypeStruct((WIN * K, HALF), F32),
            jax.ShapeDtypeStruct((MSG, 2 * TOK), BF16),
            jax.ShapeDtypeStruct((2 * TOK, HALF), BF16),
        ],
        in_specs=[pl.BlockSpec(memory_space=pltpu.HBM)] * 5,
        out_specs=[vmem] * 3,
        scratch_shapes=[
            pltpu.VMEM((GROUPS, MSG, 2 * TOK), BF16),
            pltpu.VMEM((GROUPS, TOK, SLAB), BF16),
            pltpu.VMEM((GROUPS, TOK, HALF), BF16),
            pltpu.VMEM((K, 128), F32),
            pltpu.VMEM((1, 128), jnp.int32),
            pltpu.VMEM((1, TOK), jnp.int32),
            dma((5,)),
            dma((16,)), dma((16,)), dma((GROUPS,)), dma((GROUPS,)),
            dma((GROUPS,)), dma((GROUPS,)), dma((GROUPS, 4)), dma((GROUPS, 4)),
            dma((GROUPS,)), dma((GROUPS,)), dma((GROUPS,)), dma((GROUPS,)),
        ],
        compiler_params=pltpu.CompilerParams(
            collective_id=1, has_side_effects=True, vmem_limit_bytes=24 * 1024 * 1024
        ),
    )(*hbm)
    return pl.pallas_call(
        finish,
        out_shape=jax.ShapeDtypeStruct((WIN, K, WIN), BF16),
        in_specs=[vmem] * 3,
        out_specs=pl.BlockSpec(memory_space=pltpu.HBM),
        scratch_shapes=[pltpu.VMEM((WIN, K, WIN), BF16), dma((WIN // FINE,))],
        compiler_params=pltpu.CompilerParams(vmem_limit_bytes=16 * 1024 * 1024),
    )(*[pltpu.with_memory_space_constraint(v, pltpu.VMEM) for v in parts])


def solution(mesh):
    in_specs = (P("ex", "tp"), P("ex", None), P(), P(), P("ex"))
    out_specs = P("tp", None, "ex")
    return jax.shard_map(local, mesh=mesh, in_specs=in_specs, out_specs=out_specs, check_vma=False)
```
